128 devices in a mesh: gx: 8 (over x, y_hi), gy: 16 (over z, y_lo, core).
Axes of the slice: x: 4, y: 4 (y_hi: 2, y_lo: 2; y = y_hi * 2 + y_lo), z: 4, core: 2. Of those that a mesh axis runs over, the one named last changes fastest.
Arguments:
- voltages: bfloat16 [2, 2048, 122880], P(None, ('gx', 'gy')), may hold values from -6 to 6
- gains: float32 [2, 2048, 8192], P(None, ('gx', 'gy')), may hold values from -6 to 6
- delays: float32 [64, 2048], replicated, may hold values from -32 to 32
- channel_order: int32 [8, 16], replicated, may hold values from 0 to 15, each once within a row
- beam_table: int32 [64], replicated, may hold values from 0 to 63, each once
Outputs:
- beam_power: float32 [64, 4, 8192], P('gy', None, 'gx')
The draws below stay inside these ranges and needn't reach their ends.
Inputs may be any that keep to these rules, and one draw needn't show every extreme that they name: Each row names every index of gy once; channel block a * 16 + channel_order[a, b] of 64 channels belongs to the device at gx = a, gy = b. Names every beam once; the beams beam_table[g * 64 / 16] onward, 64 / 16 of them, belong to gy index g.
All inputs are finite; a program needn't handle non-finite values.
Results may differ from the reference program's by a relative error of at most 0.009.
Values may be sent and summed in bfloat16 or wider, within the bound.
A program may use at most 128 MiB of HBM per device.

```python
import math
import jax
import jax.numpy as jnp
from jax import lax

NIN = 2048
NCH = 8192
NBEAM = 64
TAPS = 8
INTEG = 2
NSPEC = 8
SAMPLES = 122880
TIMES = 4
N_GX = 8
N_GY = 16


def levels(own_key, shape, pieces, low, top_value):
    gain = 1.0
    for axis_at, shards_of in pieces:
        heights = jax.random.uniform(jax.random.fold_in(jax.random.fold_in(own_key, 6), axis_at), (shards_of,), jnp.float32, low / len(pieces), top_value / len(pieces))
        gain = gain * jnp.repeat(jnp.exp(heights), shape[axis_at] // shards_of).reshape((-1,) + (1,) * (len(shape) - 1 - axis_at))
    return gain


def gaussian(rng, dims, spread, most, split=(), kind=jnp.bfloat16):
    array = jax.random.normal(rng, dims, jnp.float32) * spread
    if len(split) > 0:
        array = levels(rng, dims, split, -0.22, 0.18) * array
    return jnp.clip(array, min=-most, max=most).astype(kind)


def setup_inputs(seed: int = 0) -> dict:
    splits = jax.random.split(jax.random.key(seed), 6)
    voltages = gaussian(splits[0], (2, NIN, SAMPLES), 1.0, 6.0, ((1, 128),))
    gains = gaussian(splits[1], (2, NIN, NCH), 1.0, 6.0, ((1, 128),), jnp.float32)
    delays = jnp.clip(jax.random.uniform(splits[2], (NBEAM, NIN), jnp.float32, -32.0, 32.0), -32.0, 32.0)
    channel_order = jax.vmap(lambda own: jax.random.permutation(own, N_GY))(jax.random.split(splits[3], N_GX)).reshape((N_GX, N_GY)).astype(jnp.int32)
    beam_table = jax.random.permutation(splits[4], NBEAM).astype(jnp.int32)
    return {"voltages": voltages, "gains": gains, "delays": delays, "channel_order": channel_order, "beam_table": beam_table}


def coefficients():
    total = TAPS * NCH
    index = jnp.arange(total, dtype=jnp.float32)
    offset = (index - total / 2) / NCH
    window = 0.5 - 0.5 * jnp.cos(2.0 * math.pi * index / total)
    raw = jnp.sinc(offset) * window
    raw = raw / jnp.sqrt(jnp.sum(raw * raw) / NCH)
    return raw.reshape(TAPS, NCH)

def transform(filtered):
    highest = lax.Precision.HIGHEST
    first_len = 64
    second_len = NCH // first_len
    first_ids = jnp.arange(first_len, dtype=jnp.int32)
    second_ids = jnp.arange(second_len, dtype=jnp.int32)
    small_angle = 2.0 * math.pi / first_len * (first_ids[:, None] * first_ids[None, :] % first_len).astype(jnp.float32)
    small_cos = jnp.cos(small_angle)
    small_sin = -jnp.sin(small_angle)
    small_stack = jnp.concatenate([jnp.concatenate([small_cos, -small_sin], axis=1), jnp.concatenate([small_sin, small_cos], axis=1)], axis=0)
    small_stack = small_stack.astype(jnp.bfloat16).astype(jnp.float32)
    twist_angle = 2.0 * math.pi / NCH * (first_ids[:, None] * second_ids[None, :]).astype(jnp.float32)
    twist_cos = jnp.cos(twist_angle)
    twist_sin = -jnp.sin(twist_angle)
    large_angle = 2.0 * math.pi / second_len * (second_ids[:, None] * second_ids[None, :] % second_len).astype(jnp.float32)
    large_cos = jnp.cos(large_angle)
    large_sin = -jnp.sin(large_angle)
    large_stack = jnp.concatenate([jnp.concatenate([large_cos, large_sin], axis=1), jnp.concatenate([-large_sin, large_cos], axis=1)], axis=0)
    large_stack = large_stack.astype(jnp.bfloat16).astype(jnp.float32)
    inputs_here = filtered.shape[1]
    spectra_here = filtered.shape[2]
    stacked = jnp.transpose(filtered.reshape(2, inputs_here, spectra_here, first_len, second_len), (1, 2, 0, 3, 4)).reshape(inputs_here, spectra_here, 2 * first_len, second_len).astype(jnp.float32)
    inner = jnp.einsum('km,ismq->iskq', small_stack, stacked, precision=highest)
    inner_real = inner[:, :, :first_len]
    inner_imag = inner[:, :, first_len:]
    turned_real = inner_real * twist_cos - inner_imag * twist_sin
    turned_imag = inner_real * twist_sin + inner_imag * twist_cos
    turned = jnp.concatenate([turned_real, turned_imag], axis=3).astype(jnp.bfloat16).astype(jnp.float32)
    outer = jnp.einsum('iskq,qn->isnk', turned, large_stack, precision=highest)
    scale = NCH ** (-0.5)
    outer_real = outer[:, :, :second_len].reshape(inputs_here, spectra_here, NCH) * scale
    outer_imag = outer[:, :, second_len:].reshape(inputs_here, spectra_here, NCH) * scale
    return (outer_real, outer_imag)

def reference(voltages, gains, delays, channel_order, beam_table):
    taps_table = coefficients()

    def channelize(inputs):
        samples, calib = inputs
        frames = samples.reshape(2, NSPEC + TAPS - 1, NCH)
        filtered = taps_table[0] * frames[:, 0:NSPEC].astype(jnp.float32)
        for tap_index in range(1, TAPS):
            filtered = filtered + taps_table[tap_index] * frames[:, tap_index:tap_index + NSPEC].astype(jnp.float32)
        filtered = filtered.astype(jnp.bfloat16)
        spec_real, spec_imag = transform(filtered[:, None])
        spec_real = spec_real[0]
        spec_imag = spec_imag[0]
        out_real = calib[0] * spec_real - calib[1] * spec_imag
        out_imag = calib[0] * spec_imag + calib[1] * spec_real
        return jnp.stack([out_real, out_imag]).astype(jnp.bfloat16)
    spectra = lax.map(channelize, (jnp.moveaxis(voltages, 1, 0), jnp.moveaxis(gains, 1, 0)))
    offsets = jnp.take(delays, beam_table, axis=0)
    block_channels = 64
    scale = NIN ** (-0.5)

    def beam_group(group_index):
        start = group_index * block_channels
        piece = lax.dynamic_slice_in_dim(spectra, start, block_channels, 3).astype(jnp.float32)
        channel = (start + jnp.arange(block_channels, dtype=jnp.int32)).astype(jnp.float32)
        phase = channel[:, None, None] * offsets[None] * (-2.0 * math.pi / NCH)
        weight_real = (jnp.cos(phase) * scale).astype(jnp.bfloat16).astype(jnp.float32)
        weight_imag = (jnp.sin(phase) * scale).astype(jnp.bfloat16).astype(jnp.float32)
        first = jnp.einsum('cbi,ipsc->cbps', weight_real, piece)
        second = jnp.einsum('cbi,ipsc->cbps', weight_imag, piece)
        beam_real = (first[:, :, 0] - second[:, :, 1]).astype(jnp.bfloat16).astype(jnp.float32)
        beam_imag = (first[:, :, 1] + second[:, :, 0]).astype(jnp.bfloat16).astype(jnp.float32)
        power = beam_real * beam_real + beam_imag * beam_imag
        return power.reshape(block_channels, NBEAM, TIMES, INTEG).sum(axis=3)
    groups = lax.map(beam_group, jnp.arange(NCH // block_channels, dtype=jnp.int32))
    natural = jnp.transpose(groups.reshape(NCH, NBEAM, TIMES), (1, 2, 0))
    devices = N_GX * N_GY
    width = NCH // devices
    order = (jnp.arange(N_GX, dtype=jnp.int32)[:, None] * N_GY + channel_order).reshape(-1)
    placed = jnp.take(natural.reshape(NBEAM, TIMES, devices, width), order, axis=2)
    return placed.reshape(NBEAM, TIMES, NCH)
```

```python
import functools
import math

import jax
import jax.numpy as jnp
import numpy as np
from jax import lax
from jax.experimental import pallas as pl
from jax.experimental.pallas import tpu as pltpu
from jax.sharding import PartitionSpec as P

NIN = 2048
NCH = 8192
NBEAM = 64
TAPS = 8
INTEG = 2
NSPEC = 8
TIMES = 4
FRAMES = NSPEC + TAPS - 1
K1 = 64
Q = 128
HERE = 16
GROUPS = 4
KK = K1 // GROUPS
PIECES = 4
PIECE = NCH // PIECES
MESH = pl.DeviceIdType.MESH
F32 = jnp.float32
BF16 = jnp.bfloat16


def tables():
    n = np.arange(TAPS * NCH, dtype=np.float64)
    raw = np.sinc((n - TAPS * NCH / 2) / NCH) * (0.5 - 0.5 * np.cos(2 * np.pi * n / (TAPS * NCH)))
    coef = (raw / np.sqrt(np.sum(raw * raw) / NCH)).reshape(TAPS, NCH).astype(np.float32)
    k = np.arange(K1)
    q = np.arange(Q)
    ang = 2 * np.pi / K1 * (k[:, None] * k[None, :] % K1)
    c, s = np.cos(ang), np.sin(ang)
    first = np.block([[c, s], [-s, c]]).astype(np.float32)
    ang = 2 * np.pi / NCH * (k[:, None] * q[None, :])
    twist = np.stack([np.cos(ang), -np.sin(ang)]).astype(np.float32)
    ang = 2 * np.pi / Q * (q[:, None] * q[None, :] % Q)
    c, s = np.cos(ang), np.sin(ang)
    second = np.concatenate([c, s, -s, c], axis=1).astype(np.float32)
    col = np.arange(GROUPS * NSPEC * KK)
    chan = col // (NSPEC * KK) * KK + col % KK
    row = np.arange(256) % K1
    spread = (row[:, None] == chan[None, :]).astype(np.float32)
    return (
        jnp.asarray(coef),
        jnp.asarray(first, dtype=BF16),
        jnp.asarray(twist),
        jnp.asarray(second, dtype=BF16),
        jnp.asarray(spread, dtype=BF16),
    )


def times(a, b):
    return a[0] * b[0] - a[1] * b[1], a[0] * b[1] + a[1] * b[0]


def kernel(
    volt,
    gains_hbm,
    order,
    offsets,
    coef,
    first,
    twist,
    second,
    spread,
    out,
    gains,
    gcol,
    gsel,
    turned,
    stage,
    send,
    recv,
    power,
    landed,
    gain_sem,
    send_sem,
    recv_sem,
    psend_sem,
    precv_sem,
):
    gx = lax.axis_index("gx")
    gy = lax.axis_index("gy")
    me = gx * 16 + gy
    mx, my, mz, mc = gx // 2, (gx % 2) * 2 + (gy // 2) % 2, gy // 4, gy % 2

    barrier = pltpu.get_barrier_semaphore()

    def greet(j, carry):
        d = lax.rem(me + j, Q)
        pl.semaphore_signal(barrier, inc=1, device_id=(d // 16, d % 16), device_id_type=MESH)
        return carry

    gains_copy = pltpu.make_async_copy(gains_hbm, gains, gain_sem)

    def filterbank(frames, filt, frame_sem):
        for c in range(PIECES):
            for f in range(FRAMES):
                pltpu.make_async_copy(
                    volt.at[:, :, pl.ds(f * NCH + c * PIECE, PIECE)], frames.at[c, f], frame_sem.at[c]
                ).start()
        gains_copy.start()
        lax.fori_loop(1, Q, greet, 0)

        for c in range(PIECES):
            pltpu.make_async_copy(frames.at[c], frames.at[c], frame_sem.at[c]).wait()

            def fir(a, carry, c=c):
                here = pl.ds(pl.multiple_of(a * Q, Q), Q)
                there = pl.ds(pl.multiple_of(c * PIECE + a * Q, Q), Q)
                taps = [jnp.broadcast_to(coef[pl.ds(t, 1), there], (HERE, Q)) for t in range(TAPS)]
                for p in range(2):
                    x = [frames[c, f, p, :, here].astype(F32) for f in range(FRAMES)]
                    for s in range(NSPEC):
                        acc = taps[0] * x[s]
                        for t in range(1, TAPS):
                            acc = acc + taps[t] * x[s + t]
                        row = s * HERE * Q + p * K1 + c * (PIECE // Q) + a
                        filt[pl.ds(row, HERE, stride=Q), :] = acc
                return carry

            lax.fori_loop(0, PIECE // Q, fir, 0)

        def dft1(i, carry):
            x = [filt[pl.ds(pl.multiple_of((s * HERE + i) * Q, Q), Q), :].astype(BF16) for s in range(NSPEC)]
            x = jnp.concatenate(x, axis=1)
            inner = jnp.dot(first[...], x, preferred_element_type=F32)
            tc, ts = twist[0], twist[1]
            for s in range(NSPEC):
                re = inner[:K1, s * Q : (s + 1) * Q]
                im = inner[K1:, s * Q : (s + 1) * Q]
                tre = (re * tc - im * ts).astype(BF16)
                tim = (re * ts + im * tc).astype(BF16)
                for g in range(GROUPS):
                    rows = pl.ds(pl.multiple_of(i * Q + s * KK, KK), KK)
                    turned[g, rows, 0:Q] = tre[g * KK : (g + 1) * KK]
                    turned[g, rows, Q : 2 * Q] = tim[g * KK : (g + 1) * KK]
            return carry

        lax.fori_loop(0, HERE, dft1, 0)

    pl.run_scoped(
        filterbank,
        pltpu.VMEM((PIECES, FRAMES, 2, HERE, PIECE), BF16),
        pltpu.VMEM((NSPEC * HERE * Q, Q), F32),
        pltpu.SemaphoreType.DMA((PIECES,)),
    )

    gains_copy.wait()
    for j in range(NCH // Q):
        for p in range(2):
            gcol[pl.ds(p * HERE * K1 + j, HERE, stride=K1), :] = gains[p, :, j * Q : (j + 1) * Q]
    lane = lax.broadcasted_iota(jnp.int32, (Q, Q), 1)
    owner = order[...]
    one_hot = (owner == lane).astype(F32).astype(BF16)
    half_hot = ((owner // 2) == lane).astype(F32).astype(BF16)[:, :K1]
    parity = ((owner % 2) == lane // K1).astype(F32)
    parity = jnp.concatenate([parity, parity], axis=1)
    table = jnp.dot(one_hot, second[...], preferred_element_type=F32).astype(BF16)
    table = jnp.concatenate([table[:, : 2 * Q], table[:, 2 * Q :]], axis=0)

    def pick(i, carry):
        for p in range(2):
            g = gcol[pl.ds(pl.multiple_of((p * HERE + i) * K1, K1), K1), :] * F32(NCH**-0.5)
            hi = g.astype(BF16)
            lo = (g - hi.astype(F32)).astype(BF16)
            both = jnp.dot(half_hot, jnp.concatenate([hi, lo], axis=1), preferred_element_type=F32)
            gsel[pl.ds(pl.multiple_of(i * 2 * Q + p * Q, Q), Q), :] = (both * parity).astype(BF16)
        return carry

    lax.fori_loop(0, HERE, pick, 0)

    pl.semaphore_wait(barrier, Q - 1)

    for g in range(GROUPS):
        cols = slice(g * 2 * Q, (g + 1) * 2 * Q)

        def dft2(ii, carry, g=g):
            x = turned[g, pl.ds(pl.multiple_of(ii * 2 * Q, 2 * Q), 2 * Q), :]
            spec = lax.dot_general(table, x, (((1,), (1,)), ((), ())), preferred_element_type=F32)
            gain = jnp.dot(
                gsel[pl.ds(pl.multiple_of(ii * 4 * Q, 4 * Q), 4 * Q), :],
                spread[:, g * Q : (g + 1) * Q],
                preferred_element_type=F32,
            )
            for u in range(2):
                gr = gain[u * 2 * Q : u * 2 * Q + Q]
                gi = gain[u * 2 * Q + Q : (u + 1) * 2 * Q]
                sr = spec[:Q, u * Q : (u + 1) * Q]
                si = spec[Q:, u * Q : (u + 1) * Q]
                stage[pl.ds(ii * 2 + u, Q, stride=HERE), :] = gr * sr - gi * si
                stage[pl.ds(Q * HERE + ii * 2 + u, Q, stride=HERE), :] = gr * si + gi * sr
            return carry

        lax.fori_loop(0, HERE // 2, dft2, 0)

        def cast(r, carry, g=g):
            for p in range(2):
                rows = pl.ds(pl.multiple_of(r * Q, Q), Q)
                x = stage[pl.ds(pl.multiple_of(p * Q * HERE + r * Q, Q), Q), :]
                send[rows, (g * 2 + p) * Q : (g * 2 + p + 1) * Q] = x.astype(BF16)
            return carry

        lax.fori_loop(0, HERE, cast, 0)
        mine = pl.ds(pl.multiple_of(me * HERE, HERE), HERE)

        def hand_out(j, carry, g=g, cols=cols, mine=mine):
            jj = j // 2
            dx = jj % 4
            dy = (jj // 4 + dx) % 4
            dz = (jj // 16 + dy + mc * 2) % 4
            x, y, z, core = (mx + dx) % 4, (my + dy) % 4, (mz + dz) % 4, (mc + j % 2) % 2
            da = x * 2 + y // 2
            db = (z * 2 + y % 2) * 2 + core
            d = da * 16 + db

            @pl.when(d != me)
            def _():
                pltpu.make_async_remote_copy(
                    src_ref=send.at[pl.ds(pl.multiple_of(d * HERE, HERE), HERE), cols],
                    dst_ref=recv.at[mine, cols],
                    send_sem=send_sem.at[g],
                    recv_sem=recv_sem.at[g],
                    device_id=(da, db),
                    device_id_type=MESH,
                ).start()

            return carry

        lax.fori_loop(0, Q, hand_out, 0)
        recv[mine, cols] = send[mine, cols]

    def beamform(weights):
        centre = order[pl.ds(me, 1), :].astype(F32) * K1 + (K1 - 1) / 2

        def weigh(n, carry):
            lanes = pl.ds(pl.multiple_of(n // 4 * Q, Q), Q)
            r0 = n % 4 * 16
            step = offsets[pl.ds(pl.multiple_of(r0, 16), 16), lanes]
            phase = (step * centre) * F32(2 * math.pi / NCH)
            scale = F32(NIN**-0.5)
            mid = (jnp.cos(phase) * scale, -jnp.sin(phase) * scale)
            half = step * F32(math.pi / NCH)
            z1 = (jnp.cos(half), -jnp.sin(half))
            z2 = times(z1, z1)
            z3 = times(z2, z1)
            z5 = times(z3, z2)
            z7 = times(z5, z2)
            z8 = times(z7, z1)
            z16 = times(z8, z8)
            z24 = times(z16, z8)
            z40 = times(z24, z16)
            z56 = times(z40, z16)

            def both(a, b):
                rr, ii, ri, ir = a[0] * b[0], a[1] * b[1], a[0] * b[1], a[1] * b[0]
                return (rr - ii, ir + ri), (rr + ii, ir - ri)

            for far, zf in ((8, z8), (24, z24), (40, z40), (56, z56)):
                for sf, anchor in zip((1, -1), both(mid, zf)):
                    for near, zn in ((1, z1), (3, z3), (5, z5), (7, z7)):
                        for sn, w in zip((1, -1), both(anchor, zn)):
                            k = (K1 - 1 + sf * far + sn * near) // 2
                            for ri in range(2):
                                row = (k * 2 + ri) * NBEAM + r0
                                weights[pl.ds(pl.multiple_of(row, 16), 16), lanes] = w[ri].astype(BF16)
            return carry

        lax.fori_loop(0, NIN // Q * 4, weigh, 0)

        lane = lax.broadcasted_iota(jnp.int32, (Q, 2 * Q), 1) % KK
        srow = lax.broadcasted_iota(jnp.int32, (Q, Q), 0)
        scol = lax.broadcasted_iota(jnp.int32, (Q, Q), 1)
        made = None
        for g in range(GROUPS):
            cols = slice(g * 2 * Q, (g + 1) * 2 * Q)
            arrived = recv.at[pl.ds(0, (Q - 1) * HERE), cols]
            pltpu.make_async_copy(arrived, arrived, recv_sem.at[g]).wait()

            def form(m, acc, g=g, cols=cols):
                rows = pl.ds(pl.multiple_of(g * KK * Q + m * 4 * Q, 4 * Q), 4 * Q)
                res = jnp.dot(weights[rows, :], recv[:, cols], preferred_element_type=F32)
                for u in range(4):
                    acc = jnp.where(lane == m * 4 + u, res[u * Q : (u + 1) * Q], acc)
                return acc

            acc = lax.fori_loop(0, KK // 4, form, jnp.zeros((Q, 2 * Q), F32))
            br = (acc[:NBEAM, :Q] - acc[NBEAM:, Q:]).astype(BF16).astype(F32)
            bi = (acc[:NBEAM, Q:] + acc[NBEAM:, :Q]).astype(BF16).astype(F32)
            pw = br * br + bi * bi
            target = g % 2 * K1 + srow // (2 * KK) * KK + srow % KK
            gather = (target == scol).astype(F32)
            part = jnp.dot(pw, gather, preferred_element_type=F32, precision=lax.Precision.HIGHEST)
            made = part if g % 2 == 0 else made + part
            if g % 2:
                for b in range(16):
                    power[b * 8 + g // 2 * 4 : b * 8 + g // 2 * 4 + 4, :] = made[b * 4 : b * 4 + 4]

    pl.run_scoped(beamform, pltpu.VMEM((K1 * 2 * NBEAM, NIN), BF16))

    spot = pl.ds(pl.multiple_of(gy * 8, 8), 8)

    def deliver(j, carry):
        b = lax.rem(gy + j, 16)
        pltpu.make_async_remote_copy(
            src_ref=power.at[pl.ds(pl.multiple_of(b * 8, 8), 8), :],
            dst_ref=landed.at[spot, :],
            send_sem=psend_sem,
            recv_sem=precv_sem,
            device_id=(gx, b),
            device_id_type=MESH,
        ).start()
        return carry

    lax.fori_loop(1, 16, deliver, 0)
    landed[spot, :] = power[spot, :]
    for g in range(GROUPS):
        sent = send.at[pl.ds(0, (Q - 1) * HERE), pl.ds(g * 2 * Q, 2 * Q)]
        pltpu.make_async_copy(sent, sent, send_sem.at[g]).wait()
    pltpu.make_async_copy(power.at[0:120], power.at[0:120], psend_sem).wait()
    pltpu.make_async_copy(landed.at[0:120], landed.at[0:120], precv_sem).wait()
    out[...] = landed[...]


def body(voltages, gains, delays, channel_order, beam_table):
    along = lax.axis_size("gy")
    order = (jnp.arange(lax.axis_size("gx"), dtype=jnp.int32)[:, None] * along + channel_order).reshape(-1)
    order = jnp.broadcast_to(order[:, None], (Q, Q))
    offsets = jnp.take(delays, beam_table, axis=0)
    vmem = pl.BlockSpec(memory_space=pltpu.VMEM)
    hbm = pl.BlockSpec(memory_space=pl.ANY)
    landed = pl.pallas_call(
        kernel,
        out_shape=jax.ShapeDtypeStruct((Q, Q), F32),
        in_specs=[hbm, hbm] + [vmem] * 7,
        out_specs=vmem,
        scratch_shapes=[
            pltpu.VMEM((2, HERE, NCH), F32),
            pltpu.VMEM((2 * HERE * K1, Q), F32),
            pltpu.VMEM((HERE * 2 * Q, 2 * Q), BF16),
            pltpu.VMEM((GROUPS, HERE * Q, 2 * Q), BF16),
            pltpu.VMEM((2 * HERE * Q, Q), F32),
            pltpu.VMEM((Q * HERE, GROUPS * 2 * Q), BF16),
            pltpu.VMEM((Q * HERE, GROUPS * 2 * Q), BF16),
            pltpu.VMEM((Q, Q), F32),
            pltpu.VMEM((Q, Q), F32),
            pltpu.SemaphoreType.DMA,
            pltpu.SemaphoreType.DMA((GROUPS,)),
            pltpu.SemaphoreType.DMA((GROUPS,)),
            pltpu.SemaphoreType.DMA,
            pltpu.SemaphoreType.DMA,
        ],
        compiler_params=pltpu.CompilerParams(
            collective_id=0, has_side_effects=True, vmem_limit_bytes=60 * 2**20
        ),
    )(voltages, gains, order, offsets, *tables())
    landed = landed.reshape(16, 2, 4, 2, TIMES, KK)
    return jnp.transpose(landed, (2, 4, 0, 1, 3, 5)).reshape(NBEAM // along, TIMES, along * K1)


def solution(mesh):
    return jax.shard_map(
        body,
        mesh=mesh,
        in_specs=(P(None, ("gx", "gy"), None), P(None, ("gx", "gy"), None), P(), P(), P()),
        out_specs=P("gy", None, "gx"),
        check_vma=False,
    )
```

```python
import functools
import math

import jax
import jax.numpy as jnp
import numpy as np
from jax import lax
from jax.experimental import pallas as pl
from jax.experimental.pallas import tpu as pltpu
from jax.sharding import PartitionSpec as P

NIN = 2048
NCH = 8192
NBEAM = 64
TAPS = 8
INTEG = 2
NSPEC = 8
TIMES = 4
FRAMES = NSPEC + TAPS - 1
K1 = 64
QP = 136
HP = 24
KP = 72
Q = 128
HERE = 16
GROUPS = 4
KK = K1 // GROUPS
EARLY = 32
LATE = 2
PIECES = 4
PIECE = NCH // PIECES
MESH = pl.DeviceIdType.MESH
F32 = jnp.float32
BF16 = jnp.bfloat16


def tables():
    n = np.arange(TAPS * NCH, dtype=np.float64)
    raw = np.sinc((n - TAPS * NCH / 2) / NCH) * (0.5 - 0.5 * np.cos(2 * np.pi * n / (TAPS * NCH)))
    coef = (raw / np.sqrt(np.sum(raw * raw) / NCH)).reshape(TAPS, NCH).astype(np.float32)
    k = np.arange(K1)
    q = np.arange(Q)
    ang = 2 * np.pi / K1 * (k[:, None] * k[None, :] % K1)
    c, s = np.cos(ang), np.sin(ang)
    first = np.block([[c, s], [-s, c]]).astype(np.float32)
    ang = 2 * np.pi / NCH * (k[:, None] * q[None, :])
    twist = np.stack([np.cos(ang), -np.sin(ang)]).astype(np.float32)
    ang = 2 * np.pi / Q * (q[:, None] * q[None, :] % Q)
    c, s = np.cos(ang), np.sin(ang)
    second = np.concatenate([c, s, -s, c], axis=1).astype(np.float32)
    col = np.arange(GROUPS * NSPEC * KK)
    chan = col // (NSPEC * KK) * KK + col % KK
    row = np.arange(256) % K1
    spread = (row[:, None] == chan[None, :]).astype(np.float32)
    return (
        jnp.asarray(coef),
        jnp.asarray(first, dtype=BF16),
        jnp.asarray(twist),
        jnp.asarray(second, dtype=BF16),
        jnp.asarray(spread, dtype=BF16),
    )


def times(a, b):
    return a[0] * b[0] - a[1] * b[1], a[0] * b[1] + a[1] * b[0]


def eighth(x):
    y = x * x
    c = 1 + y * (-1 / 2 + y * (1 / 24 + y * (-1 / 720 + y * (1 / 40320))))
    s = x + x * y * (-1 / 6 + y * (1 / 120 + y * (-1 / 5040 + y * (1 / 362880))))
    return c, s


def kernel(
    volt,
    gains_hbm,
    channel_order,
    beam_table,
    delays,
    coef,
    first,
    twist,
    second,
    spread,
    out,
    gains,
    order,
    offsets,
    gcol,
    gsel,
    turned,
    stage,
    send,
    recv,
    power,
    landed,
    target,
    gain_sem,
    send_sem,
    recv_sem,
    psend_sem,
    precv_sem,
):
    gx = lax.axis_index("gx")
    gy = lax.axis_index("gy")
    me = gx * 16 + gy
    mx, my, mz, mc = gx // 2, (gx % 2) * 2 + (gy // 2) % 2, gy // 4, gy % 2

    barrier = pltpu.get_barrier_semaphore()

    def greet(a, carry):
        for b in range(16):
            pl.semaphore_signal(barrier, inc=1, device_id=(lax.rem(gx + a, 8), b), device_id_type=MESH)
        return carry

    def plan(m, carry):
        a, b = lax.div(m, 4), lax.rem(m, 4)
        for dx in range(4):
            x = lax.rem(mx + dx, 4)
            dy = lax.rem(b + dx, 4)
            y = lax.rem(my + dy, 4)
            z = lax.rem(mz + a + dy, 4)
            da = x * 2 + lax.div(y, 2)
            db = (z * 2 + lax.rem(y, 2)) * 2
            for core in range(2):
                target[0, m * 8 + dx * 2 + core] = da
                target[1, m * 8 + dx * 2 + core] = db + lax.rem(mc + core, 2)
        return carry

    gains_copy = pltpu.make_async_copy(gains_hbm, gains, gain_sem)

    def filterbank(frames, filt, frame_sem):
        gains_copy.start()
        for c in range(PIECES):
            for f in range(FRAMES):
                pltpu.make_async_copy(
                    volt.at[:, :, pl.ds(f * NCH + c * PIECE, PIECE)], frames.at[c, f], frame_sem.at[c]
                ).start()
        lax.fori_loop(1, 8, greet, 0)
        for b in range(1, 16):
            pl.semaphore_signal(barrier, inc=1, device_id=(gx, lax.rem(gy + b, 16)), device_id_type=MESH)
        lax.fori_loop(0, 16, plan, 0)
        owned = [jnp.broadcast_to(channel_order[a : a + 1, :], (16, 16)).astype(F32) + a * 16 for a in range(8)]
        owned = jnp.concatenate(owned, axis=0)
        row = lax.broadcasted_iota(jnp.int32, (Q, 16), 0) % 16
        col = lax.broadcasted_iota(jnp.int32, (Q, 16), 1)
        owned = jnp.sum(jnp.where(row == col, owned, 0.0), axis=1, keepdims=True)
        order[...] = jnp.broadcast_to(owned, (Q, Q)).astype(jnp.int32)

        for c in range(PIECES):
            pltpu.make_async_copy(frames.at[c], frames.at[c], frame_sem.at[c]).wait()

            def fir(a, carry, c=c):
                here = pl.ds(pl.multiple_of(a * Q, Q), Q)
                there = pl.ds(pl.multiple_of(c * PIECE + a * Q, Q), Q)
                taps = [jnp.broadcast_to(coef[pl.ds(t, 1), there], (HERE, Q)) for t in range(TAPS)]
                for p in range(2):
                    x = [frames[c, f, p, :, here].astype(F32) for f in range(FRAMES)]
                    for s in range(NSPEC):
                        acc = taps[0] * x[s]
                        for t in range(1, TAPS):
                            acc = acc + taps[t] * x[s + t]
                        row = s * HERE * QP + p * K1 + c * (PIECE // Q) + a
                        filt[pl.ds(row, HERE, stride=QP), :] = acc
                return carry

            lax.fori_loop(0, PIECE // Q, fir, 0)

        def dft1(n, carry):
            tc, ts = twist[0], twist[1]
            for i in (n * 2, n * 2 + 1):
                for s2 in range(0, NSPEC, 2):
                    x = [
                        filt[pl.ds(pl.multiple_of((s * HERE + i) * QP, 8), Q), :].astype(BF16)
                        for s in (s2, s2 + 1)
                    ]
                    inner = jnp.dot(first[...], jnp.concatenate(x, axis=1), preferred_element_type=F32)
                    for s in range(2):
                        re = inner[:K1, s * Q : (s + 1) * Q]
                        im = inner[K1:, s * Q : (s + 1) * Q]
                        tre = (re * tc - im * ts).astype(BF16)
                        tim = (re * ts + im * tc).astype(BF16)
                        for g in range(GROUPS):
                            rows = pl.ds(pl.multiple_of(i * Q + (s2 + s) * KK, KK), KK)
                            turned[g, rows, 0:Q] = tre[g * KK : (g + 1) * KK]
                            turned[g, rows, Q : 2 * Q] = tim[g * KK : (g + 1) * KK]
            return carry

        lax.fori_loop(0, HERE // 2, dft1, 0)

    pl.run_scoped(
        filterbank,
        pltpu.VMEM((PIECES, FRAMES, 2, HERE, PIECE), BF16),
        pltpu.VMEM((NSPEC * HERE * QP, Q), F32),
        pltpu.SemaphoreType.DMA((PIECES,)),
    )

    gains_copy.wait()
    for j in range(NCH // Q):
        for p in range(2):
            gcol[pl.ds(p * HERE * KP + j, HERE, stride=KP), :] = gains[p, :, j * Q : (j + 1) * Q]
    lane = lax.broadcasted_iota(jnp.int32, (Q, Q), 1)
    owner = order[...]
    one_hot = (owner == lane).astype(F32).astype(BF16)
    half_hot = ((owner // 2) == lane).astype(F32).astype(BF16)[:, :K1]
    parity = ((owner % 2) == lane // K1).astype(F32)
    parity = jnp.concatenate([parity, parity], axis=1)
    table = jnp.dot(one_hot, second[...], preferred_element_type=F32).astype(BF16)
    table = jnp.concatenate([table[:, : 2 * Q], table[:, 2 * Q :]], axis=0)

    def pick(n, carry):
        for i in range(4):
            for p in range(2):
                at = pl.multiple_of((p * HERE + n * 4 + i) * KP, 8)
                g = gcol[pl.ds(at, K1), :] * F32(NCH**-0.5)
                hi = g.astype(BF16)
                lo = (g - hi.astype(F32)).astype(BF16)
                both = jnp.dot(half_hot, jnp.concatenate([hi, lo], axis=1), preferred_element_type=F32)
                at = pl.multiple_of((n * 4 + i) * 2 * Q + p * Q, Q)
                gsel[pl.ds(at, Q), :] = (both * parity).astype(BF16)
        return carry

    lax.fori_loop(0, HERE // 4, pick, 0)

    pl.semaphore_wait(barrier, Q - 1)

    mine = pl.ds(pl.multiple_of(me * HERE, HERE), HERE)

    def hand_out(g, j):
        da, db = target[0, j], target[1, j]
        cols = pl.ds(pl.multiple_of(g * 2 * Q, 2 * Q), 2 * Q)
        pltpu.make_async_remote_copy(
            src_ref=send.at[pl.ds(pl.multiple_of((da * 16 + db) * HERE, HERE), HERE), cols],
            dst_ref=recv.at[mine, cols],
            send_sem=send_sem.at[g],
            recv_sem=recv_sem.at[g],
            device_id=(da, db),
            device_id_type=MESH,
        ).start()

    def hand_out_many(g, start, count):
        def one(j, carry):
            hand_out(g, j)
            return carry

        lax.fori_loop(jnp.maximum(start, 1), start + count, one, 0)

    for g in range(GROUPS):
        cols = slice(g * 2 * Q, (g + 1) * 2 * Q)

        def dft2(ii, carry, g=g):
            if g:
                hand_out_many(g - 1, ii * EARLY, EARLY)
            for v in range(2):
                at = ii * 2 + v
                x = turned[g, pl.ds(pl.multiple_of(at * 2 * Q, 2 * Q), 2 * Q), :]
                spec = lax.dot_general(table, x, (((1,), (1,)), ((), ())), preferred_element_type=F32)
                gain = jnp.dot(
                    gsel[pl.ds(pl.multiple_of(at * 4 * Q, 4 * Q), 4 * Q), :],
                    spread[:, g * Q : (g + 1) * Q],
                    preferred_element_type=F32,
                )
                for u in range(2):
                    gr = gain[u * 2 * Q : u * 2 * Q + Q]
                    gi = gain[u * 2 * Q + Q : (u + 1) * 2 * Q]
                    sr = spec[:Q, u * Q : (u + 1) * Q]
                    si = spec[Q:, u * Q : (u + 1) * Q]
                    stage[pl.ds(at * 2 + u, Q, stride=HP), :] = gr * sr - gi * si
                    stage[pl.ds(Q * HP + at * 2 + u, Q, stride=HP), :] = gr * si + gi * sr
            return carry

        lax.fori_loop(0, HERE // 4, dft2, 0)

        def cast(r, carry, g=g):
            for p in range(2):
                for w in range(8):
                    rows = pl.ds(pl.multiple_of(r * Q + w * HERE, HERE), HERE)
                    x = stage[pl.ds(pl.multiple_of(p * Q * HP + (r * 8 + w) * HP, 8), HERE), :]
                    send[rows, (g * 2 + p) * Q : (g * 2 + p + 1) * Q] = x.astype(BF16)
            return carry

        lax.fori_loop(0, HERE, cast, 0)
        recv[mine, cols] = send[mine, cols]

    def beamform(weights):
        centre = order[pl.ds(me, 1), :].astype(F32) * K1 + (K1 - 1) / 2

        def beam(r, carry):
            offsets[pl.ds(r, 1), :] = delays[pl.ds(beam_table[r], 1), :]
            return carry

        lax.fori_loop(0, NBEAM, beam, 0)

        def weigh(n, carry):
            hand_out_many(GROUPS - 1, n * LATE, LATE)
            lanes = pl.ds(pl.multiple_of(n // 4 * Q, Q), Q)
            r0 = n % 4 * 16
            step = offsets[pl.ds(pl.multiple_of(r0, 16), 16), lanes]
            turns = step * centre * F32(1 / NCH)
            mid = eighth((turns - jnp.round(turns)) * F32(-2 * math.pi / 8))
            mid = times(mid, mid)
            mid = times(mid, mid)
            mid = times(mid, mid)
            mid = (mid[0] * F32(NIN**-0.5), mid[1] * F32(NIN**-0.5))
            z1 = eighth(step * F32(-math.pi / NCH))
            z2 = times(z1, z1)
            z3 = times(z2, z1)
            z5 = times(z3, z2)
            z7 = times(z5, z2)
            z8 = times(z7, z1)
            z16 = times(z8, z8)
            z24 = times(z16, z8)
            z40 = times(z24, z16)
            z56 = times(z40, z16)

            def both(a, b):
                rr, ii, ri, ir = a[0] * b[0], a[1] * b[1], a[0] * b[1], a[1] * b[0]
                return (rr - ii, ir + ri), (rr + ii, ir - ri)

            for far, zf in ((8, z8), (24, z24), (40, z40), (56, z56)):
                for sf, anchor in zip((1, -1), both(mid, zf)):
                    for near, zn in ((1, z1), (3, z3), (5, z5), (7, z7)):
                        for sn, w in zip((1, -1), both(anchor, zn)):
                            k = (K1 - 1 + sf * far + sn * near) // 2
                            for ri in range(2):
                                row = (k * 2 + ri) * NBEAM + r0
                                weights[pl.ds(pl.multiple_of(row, 16), 16), lanes] = w[ri].astype(BF16)
            return carry

        lax.fori_loop(0, NIN // Q * 4, weigh, 0)

        lane = lax.broadcasted_iota(jnp.int32, (Q, 2 * Q), 1) % KK
        srow = lax.broadcasted_iota(jnp.int32, (Q, TIMES * Q), 0)
        scol = lax.broadcasted_iota(jnp.int32, (Q, TIMES * Q), 1)
        same_time = srow // (INTEG * KK) == scol // Q
        made = jnp.zeros((NBEAM, TIMES * Q), F32)
        for g in range(GROUPS):
            cols = slice(g * 2 * Q, (g + 1) * 2 * Q)
            arrived = recv.at[pl.ds(0, (Q - 1) * HERE), cols]
            pltpu.make_async_copy(arrived, arrived, recv_sem.at[g]).wait()

            def form(m, acc, g=g, cols=cols):
                rows = pl.ds(pl.multiple_of(g * KK * Q + m * 8 * Q, 8 * Q), 8 * Q)
                res = jnp.dot(weights[rows, :], recv[:, cols], preferred_element_type=F32)
                for u in range(8):
                    acc = jnp.where(lane == m * 8 + u, res[u * Q : (u + 1) * Q], acc)
                return acc

            acc = lax.fori_loop(0, KK // 8, form, jnp.zeros((Q, 2 * Q), F32))
            br = (acc[:NBEAM, :Q] - acc[NBEAM:, Q:]).astype(BF16).astype(F32)
            bi = (acc[:NBEAM, Q:] + acc[NBEAM:, :Q]).astype(BF16).astype(F32)
            pw = br * br + bi * bi
            gather = (same_time & (srow % KK + g * KK == scol % K1)).astype(F32)
            made += jnp.dot(pw, gather, preferred_element_type=F32, precision=lax.Precision.HIGHEST)
        for t in range(TIMES):
            power[pl.ds(t, NBEAM, stride=TIMES), :] = made[:, t * Q : (t + 1) * Q]

    pl.run_scoped(beamform, pltpu.VMEM((K1 * 2 * NBEAM, NIN), BF16))

    spot = pl.ds(pl.multiple_of(gy * 16, 16), 16)

    def deliver(j, carry):
        b = lax.rem(gy + j, 16)
        pltpu.make_async_remote_copy(
            src_ref=power.at[pl.ds(pl.multiple_of(b * 16, 16), 16), :],
            dst_ref=landed.at[spot, :],
            send_sem=psend_sem,
            recv_sem=precv_sem,
            device_id=(gx, b),
            device_id_type=MESH,
        ).start()
        return carry

    lax.fori_loop(1, 16, deliver, 0)
    landed[spot, :] = power[spot, :]
    for g in range(GROUPS):
        sent = send.at[pl.ds(0, (Q - 1) * HERE), pl.ds(g * 2 * Q, 2 * Q)]
        pltpu.make_async_copy(sent, sent, send_sem.at[g]).wait()
    pltpu.make_async_copy(power.at[0:240], power.at[0:240], psend_sem).wait()
    pltpu.make_async_copy(landed.at[0:240], landed.at[0:240], precv_sem).wait()
    low = lax.broadcasted_iota(jnp.int32, (16, Q), 1) < K1
    for b in range(0, 16, 2):
        pair = jnp.where(low, landed[b * 16 : b * 16 + 16, :], landed[b * 16 + 16 : b * 16 + 32, :])
        for r in range(NBEAM // 16):
            out[r, :, b * K1 : (b + 2) * K1] = pair[r * TIMES : (r + 1) * TIMES]


def body(voltages, gains, delays, channel_order, beam_table):
    vmem = pl.BlockSpec(memory_space=pltpu.VMEM)
    hbm = pl.BlockSpec(memory_space=pl.ANY)
    return pl.pallas_call(
        kernel,
        out_shape=jax.ShapeDtypeStruct((NBEAM // 16, TIMES, 16 * K1), F32),
        in_specs=[hbm, hbm, vmem, pl.BlockSpec(memory_space=pltpu.SMEM)] + [vmem] * 6,
        out_specs=vmem,
        scratch_shapes=[
            pltpu.VMEM((2, HERE, NCH), F32),
            pltpu.VMEM((Q, Q), jnp.int32),
            pltpu.VMEM((NBEAM, NIN), F32),
            pltpu.VMEM((2 * HERE * KP, Q), F32),
            pltpu.VMEM((HERE * 2 * Q, 2 * Q), BF16),
            pltpu.VMEM((GROUPS, HERE * Q, 2 * Q), BF16),
            pltpu.VMEM((2 * HP * Q, Q), F32),
            pltpu.VMEM((Q * HERE, GROUPS * 2 * Q), BF16),
            pltpu.VMEM((Q * HERE, GROUPS * 2 * Q), BF16),
            pltpu.VMEM((16 * 16, Q), F32),
            pltpu.VMEM((16 * 16, Q), F32),
            pltpu.SMEM((2, Q), jnp.int32),
            pltpu.SemaphoreType.DMA,
            pltpu.SemaphoreType.DMA((GROUPS,)),
            pltpu.SemaphoreType.DMA((GROUPS,)),
            pltpu.SemaphoreType.DMA,
            pltpu.SemaphoreType.DMA,
        ],
        compiler_params=pltpu.CompilerParams(
            collective_id=0, has_side_effects=True, vmem_limit_bytes=60 * 2**20
        ),
    )(voltages, gains, channel_order, beam_table, delays, *tables())


def solution(mesh):
    return jax.shard_map(
        body,
        mesh=mesh,
        in_specs=(P(None, ("gx", "gy"), None), P(None, ("gx", "gy"), None), P(), P(), P()),
        out_specs=P("gy", None, "gx"),
        check_vma=False,
    )
```

```python
import functools
import math

import jax
import jax.numpy as jnp
import numpy as np
from jax import lax
from jax.experimental import pallas as pl
from jax.experimental.pallas import tpu as pltpu
from jax.sharding import PartitionSpec as P

NIN = 2048
NCH = 8192
NBEAM = 64
TAPS = 8
INTEG = 2
NSPEC = 8
TIMES = 4
FRAMES = NSPEC + TAPS - 1
K1 = 64
QP = 136
HP = 24
KP = 72
Q = 128
HERE = 16
GROUPS = 4
KK = K1 // GROUPS
EARLY = 64
LATE = 2
PIECES = 4
PIECE = NCH // PIECES
MESH = pl.DeviceIdType.MESH
F32 = jnp.float32
BF16 = jnp.bfloat16


def tables():
    n = np.arange(TAPS * NCH, dtype=np.float64)
    raw = np.sinc((n - TAPS * NCH / 2) / NCH) * (0.5 - 0.5 * np.cos(2 * np.pi * n / (TAPS * NCH)))
    coef = (raw / np.sqrt(np.sum(raw * raw) / NCH)).reshape(TAPS, NCH).astype(np.float32)
    k = np.arange(K1)
    q = np.arange(Q)
    ang = 2 * np.pi / K1 * (k[:, None] * k[None, :] % K1)
    c, s = np.cos(ang), np.sin(ang)
    first = np.block([[c, s], [-s, c]]).astype(np.float32)
    first = first.reshape(2, GROUPS, KK, 2 * K1).transpose(1, 0, 2, 3).reshape(2 * K1, 2 * K1)
    ang = 2 * np.pi / NCH * (k[:, None] * q[None, :])
    twist = np.stack([np.cos(ang), -np.sin(ang)]).astype(np.float32)
    ang = 2 * np.pi / Q * (q[:, None] * q[None, :] % Q)
    c, s = np.cos(ang), np.sin(ang)
    second = np.concatenate([c, s, -s, c], axis=1).astype(np.float32)
    col = np.arange(GROUPS * NSPEC * KK)
    chan = col // (NSPEC * KK) * KK + col % KK
    row = np.arange(256) % K1
    spread = (row[:, None] == chan[None, :]).astype(np.float32)
    return (
        jnp.asarray(coef),
        jnp.asarray(first, dtype=BF16),
        jnp.asarray(twist),
        jnp.asarray(second, dtype=BF16),
        jnp.asarray(spread, dtype=BF16),
    )


def times(a, b):
    return a[0] * b[0] - a[1] * b[1], a[0] * b[1] + a[1] * b[0]


def eighth(x):
    y = x * x
    c = 1 + y * (-1 / 2 + y * (1 / 24 + y * (-1 / 720 + y * (1 / 40320))))
    s = x + x * y * (-1 / 6 + y * (1 / 120 + y * (-1 / 5040 + y * (1 / 362880))))
    return c, s


def offsets_in_order():
    order = [(dx, (b + dx) % 4, (a + b + dx) % 4, core) for a in range(4) for b in range(4) for dx in range(4) for core in range(2)]
    return order[1:]


def kernel(
    volt,
    gains_hbm,
    channel_order,
    beam_table,
    delays,
    coef,
    first,
    twist,
    second,
    spread,
    out,
    gains,
    order,
    offsets,
    gcol,
    gsel,
    turned,
    table,
    stage,
    send,
    recv,
    power,
    landed,
    target,
    gain_sem,
    send_sem,
    recv_sem,
    psend_sem,
    precv_sem,
):
    gx = lax.axis_index("gx")
    gy = lax.axis_index("gy")
    me = gx * 16 + gy
    mx, my, mz, mc = gx // 2, (gx % 2) * 2 + (gy // 2) % 2, gy // 4, gy % 2

    barrier = pltpu.get_barrier_semaphore()

    def greet(a, b):
        pl.semaphore_signal(barrier, inc=1, device_id=(a, b), device_id_type=MESH)

    def plan():
        xs = [lax.rem(mx + d, 4) * 2 for d in range(4)]
        ys = [lax.rem(my + d, 4) for d in range(4)]
        zs = [lax.rem(mz + d, 4) * 4 for d in range(4)]
        tops = [lax.div(y, 2) for y in ys]
        lows = [lax.rem(y, 2) * 2 for y in ys]
        cores = [mc, 1 - mc]
        for j, (dx, dy, dz, core) in enumerate(offsets_in_order()):
            target[0, j] = xs[dx] + tops[dy]
            target[1, j] = zs[dz] + lows[dy] + cores[core]

    mine = pl.ds(pl.multiple_of(me * HERE, HERE), HERE)

    def hand_out(g, j):
        da, db = target[0, j], target[1, j]
        cols = pl.ds(pl.multiple_of(g * 2 * Q, 2 * Q), 2 * Q)
        pltpu.make_async_remote_copy(
            src_ref=send.at[pl.ds(pl.multiple_of((da * 16 + db) * HERE, HERE), HERE), cols],
            dst_ref=recv.at[mine, cols],
            send_sem=send_sem.at[g],
            recv_sem=recv_sem.at[g],
            device_id=(da, db),
            device_id_type=MESH,
        ).start()

    def hand_out_many(g, start, count):
        def one(j, carry):
            hand_out(g, j)
            return carry

        lax.fori_loop(start, jnp.minimum(start + count, Q - 1), one, 0)

    def prepare(g):
        cols = slice(g * 2 * Q, (g + 1) * 2 * Q)

        def dft2(ii, carry):
            if g > 1:
                hand_out_many(g - 1, ii * EARLY, EARLY)
            for v in range(4):
                at = ii * 4 + v
                x = turned[g, pl.ds(pl.multiple_of(at * 2 * Q, 2 * Q), 2 * Q), :]
                spec = lax.dot_general(table[...], x, (((1,), (1,)), ((), ())), preferred_element_type=F32)
                gain = jnp.dot(
                    gsel[pl.ds(pl.multiple_of(at * 4 * Q, 4 * Q), 4 * Q), :],
                    spread[:, g * Q : (g + 1) * Q],
                    preferred_element_type=F32,
                )
                for u in range(2):
                    gr = gain[u * 2 * Q : u * 2 * Q + Q]
                    gi = gain[u * 2 * Q + Q : (u + 1) * 2 * Q]
                    sr = spec[:Q, u * Q : (u + 1) * Q]
                    si = spec[Q:, u * Q : (u + 1) * Q]
                    stage[pl.ds(at * 2 + u, Q, stride=HP), :] = gr * sr - gi * si
                    stage[pl.ds(Q * HP + at * 2 + u, Q, stride=HP), :] = gr * si + gi * sr
            return carry

        lax.fori_loop(0, HERE // 8, dft2, 0)

        def cast(r, carry):
            for p in range(2):
                for w in range(8):
                    rows = pl.ds(pl.multiple_of(r * Q + w * HERE, HERE), HERE)
                    x = stage[pl.ds(pl.multiple_of(p * Q * HP + (r * 8 + w) * HP, 8), HERE), :]
                    send[rows, (g * 2 + p) * Q : (g * 2 + p + 1) * Q] = x.astype(BF16)
            return carry

        lax.fori_loop(0, HERE, cast, 0)
        recv[mine, cols] = send[mine, cols]

    gains_copy = pltpu.make_async_copy(gains_hbm, gains, gain_sem)

    def filterbank(frames, filt, frame_sem):
        gains_copy.start()
        for c in range(PIECES):
            for f in range(FRAMES):
                pltpu.make_async_copy(
                    volt.at[:, :, pl.ds(f * NCH + c * PIECE, PIECE)], frames.at[c, f], frame_sem.at[c]
                ).start()
        for b in range(1, 16):
            greet(gx, lax.rem(gy + b, 16))

        def greet_far(far, carry):
            for b in range(16):
                greet(lax.rem(gx + far, 8), b)
            return carry

        lax.fori_loop(1, 8, greet_far, 0)
        plan()
        owned = [jnp.broadcast_to(channel_order[a : a + 1, :], (16, 16)).astype(F32) + a * 16 for a in range(8)]
        owned = jnp.concatenate(owned, axis=0)
        row = lax.broadcasted_iota(jnp.int32, (Q, 16), 0) % 16
        col = lax.broadcasted_iota(jnp.int32, (Q, 16), 1)
        owned = jnp.sum(jnp.where(row == col, owned, 0.0), axis=1, keepdims=True)
        order[...] = jnp.broadcast_to(owned, (Q, Q)).astype(jnp.int32)

        gains_copy.wait()
        for j in range(NCH // Q):
            for p in range(2):
                gcol[pl.ds(p * HERE * KP + j, HERE, stride=KP), :] = gains[p, :, j * Q : (j + 1) * Q]
        lane = lax.broadcasted_iota(jnp.int32, (Q, Q), 1)
        owner = order[...]
        half_hot = ((owner // 2) == lane).astype(F32).astype(BF16)[:, :K1]
        parity = ((owner % 2) == lane // K1).astype(F32)
        parity = jnp.concatenate([parity, parity], axis=1)
        def pick(n, carry):
            for i in range(4):
                for p in range(2):
                    at = pl.multiple_of((p * HERE + n * 4 + i) * KP, 8)
                    g = gcol[pl.ds(at, K1), :] * F32(NCH**-0.5)
                    hi = g.astype(BF16)
                    lo = (g - hi.astype(F32)).astype(BF16)
                    both = jnp.dot(half_hot, jnp.concatenate([hi, lo], axis=1), preferred_element_type=F32)
                    at = pl.multiple_of((n * 4 + i) * 2 * Q + p * Q, Q)
                    gsel[pl.ds(at, Q), :] = (both * parity).astype(BF16)
            return carry

        lax.fori_loop(0, HERE // 4, pick, 0)

        for c in range(PIECES):
            pltpu.make_async_copy(frames.at[c], frames.at[c], frame_sem.at[c]).wait()

            def fir(a, carry, c=c):
                here = pl.ds(pl.multiple_of(a * Q, Q), Q)
                there = pl.ds(pl.multiple_of(c * PIECE + a * Q, Q), Q)
                taps = [jnp.broadcast_to(coef[pl.ds(t, 1), there], (HERE, Q)).astype(BF16) for t in range(TAPS)]
                for p in range(2):
                    x = [frames[c, f, p, :, here] for f in range(FRAMES)]
                    for s in range(NSPEC):
                        terms = [taps[t] * x[s + t] for t in range(TAPS)]
                        ends = [terms[t] + terms[TAPS - 1 - t] for t in range(TAPS // 2)]
                        acc = ends[0] + ends[1] + ends[2] + ends[3]
                        row = s * HERE * QP + p * K1 + c * (PIECE // Q) + a
                        filt[pl.ds(row, HERE, stride=QP), :] = acc.astype(F32)
                return carry

            lax.fori_loop(0, PIECE // Q, fir, 0)

        def dft1(n, carry, low, high):
            if low:
                hand_out_many(0, n * (EARLY // 4), EARLY // 4)
            for i in (n * 2, n * 2 + 1):
                for s2 in range(0, NSPEC, 2):
                    x = [
                        filt[pl.ds(pl.multiple_of((s * HERE + i) * QP, 8), Q), :].astype(BF16)
                        for s in (s2, s2 + 1)
                    ]
                    x = jnp.concatenate(x, axis=1)
                    inner = jnp.dot(first[low * 2 * KK : high * 2 * KK, :], x, preferred_element_type=F32)
                    for s in range(2):
                        for g in range(low, high):
                            at = (g - low) * 2 * KK
                            re = inner[at : at + KK, s * Q : (s + 1) * Q]
                            im = inner[at + KK : at + 2 * KK, s * Q : (s + 1) * Q]
                            tc = twist[0, g * KK : (g + 1) * KK]
                            ts = twist[1, g * KK : (g + 1) * KK]
                            rows = pl.ds(pl.multiple_of(i * Q + (s2 + s) * KK, KK), KK)
                            turned[g, rows, 0:Q] = (re * tc - im * ts).astype(BF16)
                            turned[g, rows, Q : 2 * Q] = (re * ts + im * tc).astype(BF16)
            return carry

        lax.fori_loop(0, HERE // 2, functools.partial(dft1, low=0, high=1), 0)
        lane = lax.broadcasted_iota(jnp.int32, (Q, Q), 1)
        one_hot = (order[...] == lane).astype(F32).astype(BF16)
        rows = jnp.dot(one_hot, second[...], preferred_element_type=F32).astype(BF16)
        table[0:Q, :] = rows[:, : 2 * Q]
        table[Q : 2 * Q, :] = rows[:, 2 * Q :]
        pl.semaphore_wait(barrier, Q - 1)
        prepare(0)
        lax.fori_loop(0, HERE // 2, functools.partial(dft1, low=1, high=GROUPS), 0)

    pl.run_scoped(
        filterbank,
        pltpu.VMEM((PIECES, FRAMES, 2, HERE, PIECE), BF16),
        pltpu.VMEM((NSPEC * HERE * QP, Q), F32),
        pltpu.SemaphoreType.DMA((PIECES,)),
    )

    for g in range(1, GROUPS):
        prepare(g)

    def beamform(weights):
        centre = order[pl.ds(me, 1), :].astype(F32) * K1 + (K1 - 1) / 2

        def beam(r, carry):
            offsets[pl.ds(r, 1), :] = delays[pl.ds(beam_table[r], 1), :]
            return carry

        lax.fori_loop(0, NBEAM, beam, 0)

        def weigh(n, carry):
            hand_out_many(GROUPS - 1, n * LATE, LATE)
            lanes = pl.ds(pl.multiple_of(n // 4 * Q, Q), Q)
            r0 = n % 4 * 16
            step = offsets[pl.ds(pl.multiple_of(r0, 16), 16), lanes]
            turns = step * centre * F32(1 / NCH)
            mid = eighth((turns - jnp.round(turns)) * F32(-2 * math.pi / 8))
            mid = times(mid, mid)
            mid = times(mid, mid)
            mid = times(mid, mid)
            mid = (mid[0] * F32(NIN**-0.5), mid[1] * F32(NIN**-0.5))
            z1 = eighth(step * F32(-math.pi / NCH))
            z2 = times(z1, z1)
            z3 = times(z2, z1)
            z5 = times(z3, z2)
            z7 = times(z5, z2)
            z8 = times(z7, z1)
            z16 = times(z8, z8)
            z24 = times(z16, z8)
            z40 = times(z24, z16)
            z56 = times(z40, z16)

            def both(a, b):
                rr, ii, ri, ir = a[0] * b[0], a[1] * b[1], a[0] * b[1], a[1] * b[0]
                return (rr - ii, ir + ri), (rr + ii, ir - ri)

            for far, zf in ((8, z8), (24, z24), (40, z40), (56, z56)):
                for sf, anchor in zip((1, -1), both(mid, zf)):
                    for near, zn in ((1, z1), (3, z3), (5, z5), (7, z7)):
                        for sn, w in zip((1, -1), both(anchor, zn)):
                            k = (K1 - 1 + sf * far + sn * near) // 2
                            for ri in range(2):
                                row = (k * 2 + ri) * NBEAM + r0
                                weights[pl.ds(pl.multiple_of(row, 16), 16), lanes] = w[ri].astype(BF16)
            return carry

        lax.fori_loop(0, NIN // Q * 4, weigh, 0)

        lane = lax.broadcasted_iota(jnp.int32, (Q, 2 * Q), 1) % KK
        srow = lax.broadcasted_iota(jnp.int32, (Q, TIMES * Q), 0)
        scol = lax.broadcasted_iota(jnp.int32, (Q, TIMES * Q), 1)
        same_time = srow // (INTEG * KK) == scol // Q
        made = jnp.zeros((NBEAM, TIMES * Q), F32)
        for g in range(GROUPS):
            cols = slice(g * 2 * Q, (g + 1) * 2 * Q)
            arrived = recv.at[pl.ds(0, (Q - 1) * HERE), cols]
            pltpu.make_async_copy(arrived, arrived, recv_sem.at[g]).wait()

            def form(m, acc, g=g, cols=cols):
                rows = pl.ds(pl.multiple_of(g * KK * Q + m * 8 * Q, 8 * Q), 8 * Q)
                res = jnp.dot(weights[rows, :], recv[:, cols], preferred_element_type=F32)
                for u in range(8):
                    acc = jnp.where(lane == m * 8 + u, res[u * Q : (u + 1) * Q], acc)
                return acc

            acc = lax.fori_loop(0, KK // 8, form, jnp.zeros((Q, 2 * Q), F32))
            br = (acc[:NBEAM, :Q] - acc[NBEAM:, Q:]).astype(BF16).astype(F32)
            bi = (acc[:NBEAM, Q:] + acc[NBEAM:, :Q]).astype(BF16).astype(F32)
            pw = br * br + bi * bi
            gather = (same_time & (srow % KK + g * KK == scol % K1)).astype(F32)
            made += jnp.dot(pw, gather, preferred_element_type=F32, precision=lax.Precision.HIGHEST)
        for t in range(TIMES):
            power[pl.ds(t, NBEAM, stride=TIMES), :] = made[:, t * Q : (t + 1) * Q]

    pl.run_scoped(beamform, pltpu.VMEM((K1 * 2 * NBEAM, NIN), BF16))

    spot = pl.ds(pl.multiple_of(gy * 16, 16), 16)

    def deliver(j, carry):
        b = lax.rem(gy + j, 16)
        pltpu.make_async_remote_copy(
            src_ref=power.at[pl.ds(pl.multiple_of(b * 16, 16), 16), :],
            dst_ref=landed.at[spot, :],
            send_sem=psend_sem,
            recv_sem=precv_sem,
            device_id=(gx, b),
            device_id_type=MESH,
        ).start()
        return carry

    lax.fori_loop(1, 16, deliver, 0)
    landed[spot, :] = power[spot, :]
    for g in range(GROUPS):
        sent = send.at[pl.ds(0, (Q - 1) * HERE), pl.ds(g * 2 * Q, 2 * Q)]
        pltpu.make_async_copy(sent, sent, send_sem.at[g]).wait()
    pltpu.make_async_copy(power.at[0:240], power.at[0:240], psend_sem).wait()
    pltpu.make_async_copy(landed.at[0:240], landed.at[0:240], precv_sem).wait()
    low = lax.broadcasted_iota(jnp.int32, (16, Q), 1) < K1
    for b in range(0, 16, 2):
        pair = jnp.where(low, landed[b * 16 : b * 16 + 16, :], landed[b * 16 + 16 : b * 16 + 32, :])
        for r in range(NBEAM // 16):
            out[r, :, b * K1 : (b + 2) * K1] = pair[r * TIMES : (r + 1) * TIMES]


def body(voltages, gains, delays, channel_order, beam_table):
    vmem = pl.BlockSpec(memory_space=pltpu.VMEM)
    hbm = pl.BlockSpec(memory_space=pl.ANY)
    return pl.pallas_call(
        kernel,
        out_shape=jax.ShapeDtypeStruct((NBEAM // 16, TIMES, 16 * K1), F32),
        in_specs=[hbm, hbm, vmem, pl.BlockSpec(memory_space=pltpu.SMEM)] + [vmem] * 6,
        out_specs=vmem,
        scratch_shapes=[
            pltpu.VMEM((2, HERE, NCH), F32),
            pltpu.VMEM((Q, Q), jnp.int32),
            pltpu.VMEM((NBEAM, NIN), F32),
            pltpu.VMEM((2 * HERE * KP, Q), F32),
            pltpu.VMEM((HERE * 2 * Q, 2 * Q), BF16),
            pltpu.VMEM((GROUPS, HERE * Q, 2 * Q), BF16),
            pltpu.VMEM((2 * Q, 2 * Q), BF16),
            pltpu.VMEM((2 * HP * Q, Q), F32),
            pltpu.VMEM((Q * HERE, GROUPS * 2 * Q), BF16),
            pltpu.VMEM((Q * HERE, GROUPS * 2 * Q), BF16),
            pltpu.VMEM((16 * 16, Q), F32),
            pltpu.VMEM((16 * 16, Q), F32),
            pltpu.SMEM((2, Q), jnp.int32),
            pltpu.SemaphoreType.DMA,
            pltpu.SemaphoreType.DMA((GROUPS,)),
            pltpu.SemaphoreType.DMA((GROUPS,)),
            pltpu.SemaphoreType.DMA,
            pltpu.SemaphoreType.DMA,
        ],
        compiler_params=pltpu.CompilerParams(
            collective_id=0, has_side_effects=True, vmem_limit_bytes=60 * 2**20
        ),
    )(voltages, gains, channel_order, beam_table, delays, *tables())


def solution(mesh):
    return jax.shard_map(
        body,
        mesh=mesh,
        in_specs=(P(None, ("gx", "gy"), None), P(None, ("gx", "gy"), None), P(), P(), P()),
        out_specs=P("gy", None, "gx"),
        check_vma=False,
    )
```

```python
import functools
import math

import jax
import jax.numpy as jnp
import numpy as np
from jax import lax
from jax.experimental import pallas as pl
from jax.experimental.pallas import tpu as pltpu
from jax.sharding import PartitionSpec as P

NIN = 2048
NCH = 8192
NBEAM = 64
TAPS = 8
INTEG = 2
NSPEC = 8
TIMES = 4
FRAMES = NSPEC + TAPS - 1
K1 = 64
QP = 136
HP = 24
KP = 72
Q = 128
HERE = 16
GROUPS = 4
KK = K1 // GROUPS
EARLY = 64
LATE = 2
PIECES = 4
PIECE = NCH // PIECES
MESH = pl.DeviceIdType.MESH
F32 = jnp.float32
BF16 = jnp.bfloat16


def tables():
    n = np.arange(TAPS * NCH, dtype=np.float64)
    raw = np.sinc((n - TAPS * NCH / 2) / NCH) * (0.5 - 0.5 * np.cos(2 * np.pi * n / (TAPS * NCH)))
    coef = (raw / np.sqrt(np.sum(raw * raw) / NCH)).reshape(TAPS, NCH).astype(np.float32)
    k = np.arange(K1)
    q = np.arange(Q)
    ang = 2 * np.pi / K1 * (k[:, None] * k[None, :] % K1)
    c, s = np.cos(ang), np.sin(ang)
    first = np.block([[c, s], [-s, c]]).astype(np.float32)
    first = first.reshape(2, GROUPS, KK, 2 * K1).transpose(1, 0, 2, 3).reshape(2 * K1, 2 * K1)
    ang = 2 * np.pi / NCH * (k[:, None] * q[None, :])
    twist = np.stack([np.cos(ang), -np.sin(ang)]).astype(np.float32)
    ang = 2 * np.pi / Q * (q[:, None] * q[None, :] % Q)
    c, s = np.cos(ang), np.sin(ang)
    second = np.concatenate([c, s, -s, c], axis=1).astype(np.float32)
    col = np.arange(GROUPS * NSPEC * KK)
    chan = col // (NSPEC * KK) * KK + col % KK
    row = np.arange(256) % K1
    spread = (row[:, None] == chan[None, :]).astype(np.float32)
    return (
        jnp.asarray(coef),
        jnp.asarray(first, dtype=BF16),
        jnp.asarray(twist),
        jnp.asarray(second, dtype=BF16),
        jnp.asarray(spread, dtype=BF16),
    )


def times(a, b):
    return a[0] * b[0] - a[1] * b[1], a[0] * b[1] + a[1] * b[0]


def eighth(x):
    y = x * x
    c = 1 + y * (-1 / 2 + y * (1 / 24 + y * (-1 / 720 + y * (1 / 40320))))
    s = x + x * y * (-1 / 6 + y * (1 / 120 + y * (-1 / 5040 + y * (1 / 362880))))
    return c, s


def offsets_in_order():
    order = [(dx, (b + dx) % 4, (a + b + dx) % 4, core) for a in range(4) for b in range(4) for dx in range(4) for core in range(2)]
    return order[1:]


def kernel(
    volt,
    gains_hbm,
    channel_order,
    beam_table,
    delays,
    coef,
    first,
    twist,
    second,
    spread,
    out,
    gains,
    order,
    offsets,
    gcol,
    gsel,
    turned,
    table,
    stage,
    send,
    recv,
    power,
    landed,
    target,
    gain_sem,
    send_sem,
    recv_sem,
    psend_sem,
    precv_sem,
):
    gx = lax.axis_index("gx")
    gy = lax.axis_index("gy")
    me = gx * 16 + gy
    mx, my, mz, mc = gx // 2, (gx % 2) * 2 + (gy // 2) % 2, gy // 4, gy % 2

    barrier = pltpu.get_barrier_semaphore()

    def greet(a, b):
        pl.semaphore_signal(barrier, inc=1, device_id=(a, b), device_id_type=MESH)

    def plan():
        xs = [lax.rem(mx + d, 4) * 2 for d in range(4)]
        ys = [lax.rem(my + d, 4) for d in range(4)]
        zs = [lax.rem(mz + d, 4) * 4 for d in range(4)]
        tops = [lax.div(y, 2) for y in ys]
        lows = [lax.rem(y, 2) * 2 for y in ys]
        cores = [mc, 1 - mc]
        for j, (dx, dy, dz, core) in enumerate(offsets_in_order()):
            target[0, j] = xs[dx] + tops[dy]
            target[1, j] = zs[dz] + lows[dy] + cores[core]

    mine = pl.ds(pl.multiple_of(me * HERE, HERE), HERE)

    def hand_out(g, j):
        da, db = target[0, j], target[1, j]
        cols = pl.ds(pl.multiple_of(g * 2 * Q, 2 * Q), 2 * Q)
        pltpu.make_async_remote_copy(
            src_ref=send.at[pl.ds(pl.multiple_of((da * 16 + db) * HERE, HERE), HERE), cols],
            dst_ref=recv.at[mine, cols],
            send_sem=send_sem.at[g],
            recv_sem=recv_sem.at[g],
            device_id=(da, db),
            device_id_type=MESH,
        ).start()

    def hand_out_many(g, start, count):
        def one(j, carry):
            hand_out(g, j)
            return carry

        lax.fori_loop(start, jnp.minimum(start + count, Q - 1), one, 0)

    def prepare(g):
        cols = slice(g * 2 * Q, (g + 1) * 2 * Q)

        def dft2(ii, carry):
            if g > 1:
                hand_out_many(g - 1, ii * EARLY, EARLY)
            for v in range(4):
                at = ii * 4 + v
                x = turned[g, pl.ds(pl.multiple_of(at * 2 * Q, 2 * Q), 2 * Q), :]
                spec = lax.dot_general(table[...], x, (((1,), (1,)), ((), ())), preferred_element_type=F32)
                gain = jnp.dot(
                    gsel[pl.ds(pl.multiple_of(at * 4 * Q, 4 * Q), 4 * Q), :],
                    spread[:, g * Q : (g + 1) * Q],
                    preferred_element_type=F32,
                )
                for u in range(2):
                    gr = gain[u * 2 * Q : u * 2 * Q + Q]
                    gi = gain[u * 2 * Q + Q : (u + 1) * 2 * Q]
                    sr = spec[:Q, u * Q : (u + 1) * Q]
                    si = spec[Q:, u * Q : (u + 1) * Q]
                    stage[pl.ds(at * 2 + u, Q, stride=HP), :] = gr * sr - gi * si
                    stage[pl.ds(Q * HP + at * 2 + u, Q, stride=HP), :] = gr * si + gi * sr
            return carry

        lax.fori_loop(0, HERE // 8, dft2, 0)

        def cast(r, carry):
            for p in range(2):
                for w in range(8):
                    rows = pl.ds(pl.multiple_of(r * Q + w * HERE, HERE), HERE)
                    x = stage[pl.ds(pl.multiple_of(p * Q * HP + (r * 8 + w) * HP, 8), HERE), :]
                    send[rows, (g * 2 + p) * Q : (g * 2 + p + 1) * Q] = x.astype(BF16)
            return carry

        lax.fori_loop(0, HERE, cast, 0)
        recv[mine, cols] = send[mine, cols]

    gains_copy = pltpu.make_async_copy(gains_hbm, gains, gain_sem)

    def filterbank(frames, filt, frame_sem):
        gains_copy.start()
        for c in range(PIECES):
            for f in range(FRAMES):
                pltpu.make_async_copy(
                    volt.at[:, :, pl.ds(f * NCH + c * PIECE, PIECE)], frames.at[c, f], frame_sem.at[c]
                ).start()
        for b in range(1, 16):
            greet(gx, lax.rem(gy + b, 16))

        def greet_far(far, carry):
            for b in range(16):
                greet(lax.rem(gx + far, 8), b)
            return carry

        lax.fori_loop(1, 8, greet_far, 0)
        plan()
        owned = [jnp.broadcast_to(channel_order[a : a + 1, :], (16, 16)).astype(F32) + a * 16 for a in range(8)]
        owned = jnp.concatenate(owned, axis=0)
        row = lax.broadcasted_iota(jnp.int32, (Q, 16), 0) % 16
        col = lax.broadcasted_iota(jnp.int32, (Q, 16), 1)
        owned = jnp.sum(jnp.where(row == col, owned, 0.0), axis=1, keepdims=True)
        order[...] = jnp.broadcast_to(owned, (Q, Q)).astype(jnp.int32)

        gains_copy.wait()
        for j in range(NCH // Q):
            for p in range(2):
                gcol[pl.ds(p * HERE * KP + j, HERE, stride=KP), :] = gains[p, :, j * Q : (j + 1) * Q]
        lane = lax.broadcasted_iota(jnp.int32, (Q, Q), 1)
        owner = order[...]
        half_hot = ((owner // 2) == lane).astype(F32).astype(BF16)[:, :K1]
        parity = ((owner % 2) == lane // K1).astype(F32)
        parity = jnp.concatenate([parity, parity], axis=1)
        def pick(n, carry):
            for i in range(4):
                for p in range(2):
                    at = pl.multiple_of((p * HERE + n * 4 + i) * KP, 8)
                    g = gcol[pl.ds(at, K1), :] * F32(NCH**-0.5)
                    hi = g.astype(BF16)
                    lo = (g - hi.astype(F32)).astype(BF16)
                    both = jnp.dot(half_hot, jnp.concatenate([hi, lo], axis=1), preferred_element_type=F32)
                    at = pl.multiple_of((n * 4 + i) * 2 * Q + p * Q, Q)
                    gsel[pl.ds(at, Q), :] = (both * parity).astype(BF16)
            return carry

        lax.fori_loop(0, HERE // 4, pick, 0)

        for c in range(PIECES):
            pltpu.make_async_copy(frames.at[c], frames.at[c], frame_sem.at[c]).wait()

            def fir(a, carry, c=c):
                here = pl.ds(pl.multiple_of(a * Q, Q), Q)
                there = pl.ds(pl.multiple_of(c * PIECE + a * Q, Q), Q)
                taps = [jnp.broadcast_to(coef[pl.ds(t, 1), there], (HERE, Q)).astype(BF16) for t in range(TAPS)]
                for p in range(2):
                    x = [frames[c, f, p, :, here] for f in range(FRAMES)]
                    for s in range(NSPEC):
                        terms = [taps[t] * x[s + t] for t in range(TAPS)]
                        ends = [terms[t] + terms[TAPS - 1 - t] for t in range(TAPS // 2)]
                        acc = ends[0] + ends[1] + ends[2] + ends[3]
                        row = s * HERE * QP + p * K1 + c * (PIECE // Q) + a
                        filt[pl.ds(row, HERE, stride=QP), :] = acc.astype(F32)
                return carry

            lax.fori_loop(0, PIECE // Q, fir, 0)

        def dft1(n, carry, low, high):
            if low:
                hand_out_many(0, n * (EARLY // 4), EARLY // 4)
            each = 2 if low else 4
            for i in [n * each + u for u in range(each)]:
                for s2 in range(0, NSPEC, 2):
                    x = [
                        filt[pl.ds(pl.multiple_of((s * HERE + i) * QP, 8), Q), :].astype(BF16)
                        for s in (s2, s2 + 1)
                    ]
                    x = jnp.concatenate(x, axis=1)
                    inner = jnp.dot(first[low * 2 * KK : high * 2 * KK, :], x, preferred_element_type=F32)
                    for s in range(2):
                        for g in range(low, high):
                            at = (g - low) * 2 * KK
                            re = inner[at : at + KK, s * Q : (s + 1) * Q]
                            im = inner[at + KK : at + 2 * KK, s * Q : (s + 1) * Q]
                            tc = twist[0, g * KK : (g + 1) * KK]
                            ts = twist[1, g * KK : (g + 1) * KK]
                            rows = pl.ds(pl.multiple_of(i * Q + (s2 + s) * KK, KK), KK)
                            turned[g, rows, 0:Q] = (re * tc - im * ts).astype(BF16)
                            turned[g, rows, Q : 2 * Q] = (re * ts + im * tc).astype(BF16)
            return carry

        lax.fori_loop(0, HERE // 4, functools.partial(dft1, low=0, high=1), 0)
        lane = lax.broadcasted_iota(jnp.int32, (Q, Q), 1)
        one_hot = (order[...] == lane).astype(F32).astype(BF16)
        rows = jnp.dot(one_hot, second[...], preferred_element_type=F32).astype(BF16)
        table[0:Q, :] = rows[:, : 2 * Q]
        table[Q : 2 * Q, :] = rows[:, 2 * Q :]
        pl.semaphore_wait(barrier, Q - 1)
        prepare(0)
        lax.fori_loop(0, HERE // 2, functools.partial(dft1, low=1, high=GROUPS), 0)

    pl.run_scoped(
        filterbank,
        pltpu.VMEM((PIECES, FRAMES, 2, HERE, PIECE), BF16),
        pltpu.VMEM((NSPEC * HERE * QP, Q), F32),
        pltpu.SemaphoreType.DMA((PIECES,)),
    )

    for g in range(1, GROUPS):
        prepare(g)

    def beamform(weights):
        centre = order[pl.ds(me, 1), :].astype(F32) * K1 + (K1 - 1) / 2

        def beam(r, carry):
            offsets[pl.ds(r, 1), :] = delays[pl.ds(beam_table[r], 1), :]
            return carry

        lax.fori_loop(0, NBEAM, beam, 0)

        def weigh(n, carry):
            hand_out_many(GROUPS - 1, n * LATE, LATE)
            lanes = pl.ds(pl.multiple_of(n // 4 * Q, Q), Q)
            r0 = n % 4 * 16
            step = offsets[pl.ds(pl.multiple_of(r0, 16), 16), lanes]
            turns = step * centre * F32(1 / NCH)
            mid = eighth((turns - jnp.round(turns)) * F32(-2 * math.pi / 8))
            mid = times(mid, mid)
            mid = times(mid, mid)
            mid = times(mid, mid)
            mid = (mid[0] * F32(NIN**-0.5), mid[1] * F32(NIN**-0.5))
            z1 = eighth(step * F32(-math.pi / NCH))
            z2 = times(z1, z1)
            z3 = times(z2, z1)
            z5 = times(z3, z2)
            z7 = times(z5, z2)
            z8 = times(z7, z1)
            z16 = times(z8, z8)
            z24 = times(z16, z8)
            z40 = times(z24, z16)
            z56 = times(z40, z16)

            def both(a, b):
                rr, ii, ri, ir = a[0] * b[0], a[1] * b[1], a[0] * b[1], a[1] * b[0]
                return (rr - ii, ir + ri), (rr + ii, ir - ri)

            for far, zf in ((8, z8), (24, z24), (40, z40), (56, z56)):
                for sf, anchor in zip((1, -1), both(mid, zf)):
                    for near, zn in ((1, z1), (3, z3), (5, z5), (7, z7)):
                        for sn, w in zip((1, -1), both(anchor, zn)):
                            k = (K1 - 1 + sf * far + sn * near) // 2
                            for ri in range(2):
                                row = (k * 2 + ri) * NBEAM + r0
                                weights[pl.ds(pl.multiple_of(row, 16), 16), lanes] = w[ri].astype(BF16)
            return carry

        lax.fori_loop(0, NIN // Q * 4, weigh, 0)

        lane = lax.broadcasted_iota(jnp.int32, (Q, 2 * Q), 1) % KK
        srow = lax.broadcasted_iota(jnp.int32, (Q, TIMES * Q), 0)
        scol = lax.broadcasted_iota(jnp.int32, (Q, TIMES * Q), 1)
        same_time = srow // (INTEG * KK) == scol // Q
        made = jnp.zeros((NBEAM, TIMES * Q), F32)
        for g in range(GROUPS):
            cols = slice(g * 2 * Q, (g + 1) * 2 * Q)
            arrived = recv.at[pl.ds(0, (Q - 1) * HERE), cols]
            pltpu.make_async_copy(arrived, arrived, recv_sem.at[g]).wait()

            def form(m, acc, g=g, cols=cols):
                rows = pl.ds(pl.multiple_of(g * KK * Q + m * 8 * Q, 8 * Q), 8 * Q)
                res = jnp.dot(weights[rows, :], recv[:, cols], preferred_element_type=F32)
                for u in range(8):
                    acc = jnp.where(lane == m * 8 + u, res[u * Q : (u + 1) * Q], acc)
                return acc

            acc = lax.fori_loop(0, KK // 8, form, jnp.zeros((Q, 2 * Q), F32))
            br = (acc[:NBEAM, :Q] - acc[NBEAM:, Q:]).astype(BF16).astype(F32)
            bi = (acc[:NBEAM, Q:] + acc[NBEAM:, :Q]).astype(BF16).astype(F32)
            pw = br * br + bi * bi
            gather = (same_time & (srow % KK + g * KK == scol % K1)).astype(F32)
            made += jnp.dot(pw, gather, preferred_element_type=F32, precision=lax.Precision.HIGHEST)
        for t in range(TIMES):
            power[pl.ds(t, NBEAM, stride=TIMES), :] = made[:, t * Q : (t + 1) * Q]

    pl.run_scoped(beamform, pltpu.VMEM((K1 * 2 * NBEAM, NIN), BF16))

    spot = pl.ds(pl.multiple_of(gy * 16, 16), 16)

    def deliver(j, carry):
        b = lax.rem(gy + j, 16)
        pltpu.make_async_remote_copy(
            src_ref=power.at[pl.ds(pl.multiple_of(b * 16, 16), 16), :],
            dst_ref=landed.at[spot, :],
            send_sem=psend_sem,
            recv_sem=precv_sem,
            device_id=(gx, b),
            device_id_type=MESH,
        ).start()
        return carry

    lax.fori_loop(1, 16, deliver, 0)
    landed[spot, :] = power[spot, :]
    for g in range(GROUPS):
        sent = send.at[pl.ds(0, (Q - 1) * HERE), pl.ds(g * 2 * Q, 2 * Q)]
        pltpu.make_async_copy(sent, sent, send_sem.at[g]).wait()
    pltpu.make_async_copy(power.at[0:240], power.at[0:240], psend_sem).wait()
    pltpu.make_async_copy(landed.at[0:240], landed.at[0:240], precv_sem).wait()
    low = lax.broadcasted_iota(jnp.int32, (16, Q), 1) < K1
    for b in range(0, 16, 2):
        pair = jnp.where(low, landed[b * 16 : b * 16 + 16, :], landed[b * 16 + 16 : b * 16 + 32, :])
        for r in range(NBEAM // 16):
            out[r, :, b * K1 : (b + 2) * K1] = pair[r * TIMES : (r + 1) * TIMES]


def body(voltages, gains, delays, channel_order, beam_table):
    vmem = pl.BlockSpec(memory_space=pltpu.VMEM)
    hbm = pl.BlockSpec(memory_space=pl.ANY)
    return pl.pallas_call(
        kernel,
        out_shape=jax.ShapeDtypeStruct((NBEAM // 16, TIMES, 16 * K1), F32),
        in_specs=[hbm, hbm, vmem, pl.BlockSpec(memory_space=pltpu.SMEM)] + [vmem] * 6,
        out_specs=vmem,
        scratch_shapes=[
            pltpu.VMEM((2, HERE, NCH), F32),
            pltpu.VMEM((Q, Q), jnp.int32),
            pltpu.VMEM((NBEAM, NIN), F32),
            pltpu.VMEM((2 * HERE * KP, Q), F32),
            pltpu.VMEM((HERE * 2 * Q, 2 * Q), BF16),
            pltpu.VMEM((GROUPS, HERE * Q, 2 * Q), BF16),
            pltpu.VMEM((2 * Q, 2 * Q), BF16),
            pltpu.VMEM((2 * HP * Q, Q), F32),
            pltpu.VMEM((Q * HERE, GROUPS * 2 * Q), BF16),
            pltpu.VMEM((Q * HERE, GROUPS * 2 * Q), BF16),
            pltpu.VMEM((16 * 16, Q), F32),
            pltpu.VMEM((16 * 16, Q), F32),
            pltpu.SMEM((2, Q), jnp.int32),
            pltpu.SemaphoreType.DMA,
            pltpu.SemaphoreType.DMA((GROUPS,)),
            pltpu.SemaphoreType.DMA((GROUPS,)),
            pltpu.SemaphoreType.DMA,
            pltpu.SemaphoreType.DMA,
        ],
        compiler_params=pltpu.CompilerParams(
            collective_id=0, has_side_effects=True, vmem_limit_bytes=60 * 2**20
        ),
    )(voltages, gains, channel_order, beam_table, delays, *tables())


def solution(mesh):
    return jax.shard_map(
        body,
        mesh=mesh,
        in_specs=(P(None, ("gx", "gy"), None), P(None, ("gx", "gy"), None), P(), P(), P()),
        out_specs=P("gy", None, "gx"),
        check_vma=False,
    )
```
